32 devices in a mesh: ctx: 8 (over z, y), head: 4 (over x, core).
Axes of the slice: x: 2, y: 2, z: 4, core: 2. Of those that a mesh axis runs over, the one named last changes fastest.
Arguments:
- query: bfloat16 [16384, 2048], P('ctx', 'head'), may hold values from -6 to 6
- key: bfloat16 [16384, 2048], P('ctx', 'head'), may hold values from -6 to 6
- value: bfloat16 [16384, 2048], P('ctx', 'head'), may hold values from -6 to 6
- gain: bfloat16 [2048], P('head'), may hold values from 0.099609375 to 1.8984375
- w_out: bfloat16 [2048, 2048], replicated, may hold values from -0.125 to 0.125
- d_out: bfloat16 [16384, 2048], P(('ctx', 'head')), may hold values from -6 to 6
Outputs:
- out: bfloat16 [16384, 2048], P(('ctx', 'head'))
- grad_query: bfloat16 [16384, 2048], P('ctx', 'head')
- grad_key: bfloat16 [16384, 2048], P('ctx', 'head')
- grad_value: bfloat16 [16384, 2048], P('ctx', 'head')
The draws below stay inside these ranges and needn't reach their ends.
All inputs are finite; a program needn't handle non-finite values.
Results may differ from the reference program's by a relative error of at most 0.018.
Values may be sent and summed in bfloat16 or wider, within the bound.
No kernel may reach another device: no remote copies, remote signals or barrier semaphores. Data moves between devices by JAX's collectives and lax.ppermute only.
A program may use at most 128 MiB of HBM per device.

```python
import jax
import jax.numpy as jnp
from jax import lax

HEADS = 16
HDIM = 128
BLOCK = 128
D = 2048
TOKENS = 16384


def shard_levels(stream_key, shape, shards, low, largest):
    loudness = 1.0
    for axis_at, blocks in shards:
        steps = jax.random.uniform(jax.random.fold_in(jax.random.fold_in(stream_key, 6), axis_at), (blocks,), jnp.float32, low / len(shards), largest / len(shards))
        loudness = loudness * jnp.repeat(jnp.exp(steps), shape[axis_at] // blocks).reshape((-1,) + (1,) * (len(shape) - 1 - axis_at))
    return loudness


def centred(key, extent, scale, limit, pieces=(), kind=jnp.bfloat16):
    drawn = scale * jax.random.normal(key, extent, jnp.float32)
    if pieces:
        drawn = drawn * shard_levels(key, extent, pieces, -0.22, 0.18)
    return jnp.clip(drawn, -limit, limit).astype(kind)


def setup_inputs(seed: int = 0) -> dict:
    keys = jax.random.split(jax.random.key(seed), 7)
    return {
        "query": centred(keys[0], (TOKENS, D), 1.0, 6.0, ((0, 8), (1, 4))),
        "key": centred(keys[1], (TOKENS, D), 1.0, 6.0, ((0, 8), (1, 4))),
        "value": centred(keys[2], (TOKENS, D), 1.0, 6.0, ((0, 8), (1, 4))),
        "gain": jnp.clip(1.0 + 0.18 * jax.random.normal(keys[3], (D,), jnp.float32), 0.099609375, 1.8984375).astype(jnp.bfloat16),
        "w_out": centred(keys[4], (D, D), D ** -0.5, 0.125),
        "d_out": centred(keys[5], (TOKENS, D), 1.0, 6.0, ((0, 32),)),
    }


epsilon = 1e-06
highest = lax.Precision.HIGHEST

def rounded(values):
    return lax.optimization_barrier(values.astype(jnp.bfloat16)).astype(values.dtype)

def product(form, left, right):
    return jnp.einsum(form, left, right, precision=highest)

def reference(query, key, value, gain, w_out, d_out):
    nblocks = TOKENS // BLOCK
    causal = jnp.tril(jnp.ones((BLOCK, BLOCK), dtype=bool))[None]

    def split_blocks(array):
        return array.reshape(nblocks, BLOCK, HEADS, HDIM)

    def masked(scores):
        return rounded(jnp.where(causal, scores, jnp.zeros_like(scores)))
    inputs = (split_blocks(query), split_blocks(key), split_blocks(value))
    zero_state = jnp.zeros((HEADS, HDIM, HDIM), jnp.float32)

    def forward_step(state, block_in):
        q_blk, k_blk, v_blk = [piece.astype(jnp.float32) for piece in block_in]
        weights = masked(product('she,the->hst', q_blk, k_blk))
        output = product('hst,thf->shf', weights, v_blk) + product('she,hef->shf', q_blk, rounded(state))
        return (state + product('she,shf->hef', k_blk, v_blk), output)
    _, attended = lax.scan(forward_step, zero_state, inputs)
    attended = attended.reshape(TOKENS, HEADS, HDIM)
    inverse = lax.rsqrt(lax.optimization_barrier(jnp.mean(attended * attended, axis=-1, keepdims=True)) + epsilon)
    unit = attended * inverse
    scales = gain.astype(jnp.float32).reshape(HEADS, HDIM)
    normed = (unit * scales).astype(jnp.bfloat16).reshape(TOKENS, D)
    out = jnp.dot(normed, w_out, preferred_element_type=jnp.float32).astype(jnp.bfloat16)
    grad_rows = lax.dot_general(d_out, w_out, (((1,), (1,)), ((), ())), preferred_element_type=jnp.float32)
    grad_normed = rounded(grad_rows).reshape(TOKENS, HEADS, HDIM)
    grad_unit = grad_normed * scales
    grad_attended = inverse * (grad_unit - unit * lax.optimization_barrier(jnp.mean(grad_unit * unit, axis=-1, keepdims=True)))
    grad_blocks = split_blocks(grad_attended.astype(jnp.bfloat16))

    def query_step(state, block_in):
        k_blk, v_blk, g_blk = [piece.astype(jnp.float32) for piece in block_in]
        weights = masked(product('shf,thf->hst', g_blk, v_blk))
        grad_q = product('hst,the->she', weights, k_blk) + product('shf,hef->she', g_blk, rounded(state))
        return (state + product('she,shf->hef', k_blk, v_blk), grad_q)
    _, grad_query = lax.scan(query_step, zero_state, (inputs[1], inputs[2], grad_blocks))

    def key_step(later, block_in):
        q_blk, k_blk, v_blk, g_blk = [piece.astype(jnp.float32) for piece in block_in]
        weights = masked(product('shf,thf->hst', g_blk, v_blk))
        scores = masked(product('she,the->hst', q_blk, k_blk))
        frozen = rounded(later)
        grad_k = product('hst,she->the', weights, q_blk) + product('thf,hef->the', v_blk, frozen)
        grad_v = product('hst,shf->thf', scores, g_blk) + product('the,hef->thf', k_blk, frozen)
        return (later + product('she,shf->hef', q_blk, g_blk), (grad_k, grad_v))
    _, (grad_key, grad_value) = lax.scan(key_step, zero_state, inputs + (grad_blocks,), reverse=True)
    return (out, grad_query.reshape(TOKENS, D).astype(jnp.bfloat16), grad_key.reshape(TOKENS, D).astype(jnp.bfloat16), grad_value.reshape(TOKENS, D).astype(jnp.bfloat16))
```

```python
import functools

import jax
import jax.numpy as jnp
from jax import lax
from jax.experimental import pallas as pl
from jax.experimental.pallas import tpu as pltpu
from jax.sharding import PartitionSpec as P

HDIM = 128
BLOCK = 128
epsilon = 1e-06
f32 = jnp.float32
bf16 = jnp.bfloat16
MIB = 1 << 20


def mm(a, b, ca, cb):
    return lax.dot_general(a, b, (((ca,), (cb,)), ((), ())), preferred_element_type=f32)


def params(mib, dims=1):
    return pltpu.CompilerParams(
        vmem_limit_bytes=mib * MIB, dimension_semantics=("arbitrary",) * dims
    )


def keep_causal(scores):
    row = lax.broadcasted_iota(jnp.int32, (BLOCK, BLOCK), 0)
    col = lax.broadcasted_iota(jnp.int32, (BLOCK, BLOCK), 1)
    return jnp.where(col <= row, scores, 0.0).astype(bf16)


def grad_rows_kernel(npieces, me_ref, d_ref, *refs):
    w_refs, o_refs, acc_refs = refs[:npieces], refs[npieces : 2 * npieces], refs[2 * npieces :]
    step, last = pl.program_id(0), pl.num_programs(0) - 1
    for w_ref, o_ref, acc_ref in zip(w_refs, o_refs, acc_refs):
        part = mm(d_ref[...], w_ref[...], 1, 1)

        @pl.when(step == 0)
        def _():
            acc_ref[...] = part

        @pl.when((step > 0) & (step < last))
        def _():
            acc_ref[...] += part

        @pl.when(step == last)
        def _():
            o_ref[...] = (acc_ref[...] + part).astype(bf16)


def grad_rows(me, d_out, w_out, pieces, chunks, cols):
    rows, model = d_out.shape
    tile = min(512, model)
    n = len(pieces)

    def w_spec(dist, chunk):
        return pl.BlockSpec((cols, tile), lambda k, m: ((m[0] ^ dist) * chunks + chunk, k))

    return pl.pallas_call(
        functools.partial(grad_rows_kernel, n),
        grid_spec=pltpu.PrefetchScalarGridSpec(
            num_scalar_prefetch=1,
            grid=(model // tile,),
            in_specs=[pl.BlockSpec((rows, tile), lambda k, m: (0, k))]
            + [w_spec(*piece) for piece in pieces],
            out_specs=[pl.BlockSpec((rows, cols), lambda k, m: (0, 0))] * n,
            scratch_shapes=[pltpu.VMEM((rows, cols), f32)] * n,
        ),
        out_shape=[jax.ShapeDtypeStruct((rows, cols), bf16)] * n,
        compiler_params=params(24),
        name="grad_rows",
    )(me, d_out, *([w_out] * n))


def total_kernel(k_ref, v_ref, o_ref):
    @pl.when(pl.program_id(0) == 0)
    def _():
        o_ref[...] = jnp.zeros_like(o_ref)

    for h in range(o_ref.shape[0]):
        cols = slice(h * HDIM, (h + 1) * HDIM)
        o_ref[h] += mm(k_ref[:, cols], v_ref[:, cols], 0, 0)


def total_state(key, value):
    tokens, width = key.shape
    tile = min(512, tokens)
    spec = pl.BlockSpec((tile, width), lambda i: (i, 0))
    heads = width // HDIM
    return pl.pallas_call(
        total_kernel,
        grid=(tokens // tile,),
        in_specs=[spec, spec],
        out_specs=pl.BlockSpec((heads, HDIM, HDIM), lambda i: (0, 0, 0)),
        out_shape=jax.ShapeDtypeStruct((heads, HDIM, HDIM), f32),
        compiler_params=params(24),
        name="total_state",
    )(key, value)


def forward_kernel(nhead, me_ref, q_ref, k_ref, v_ref, gain_ref, before_ref, *refs):
    n_refs = refs[:nhead]
    att_ref, s_ref, st_ref, run_ref, row_ref = refs[nhead:]
    step = pl.program_id(0)
    heads = before_ref.shape[0]

    @pl.when(step == 0)
    def _():
        run_ref[...] = before_ref[...]

    for h in range(heads):
        cols = slice(h * HDIM, (h + 1) * HDIM)
        gain = gain_ref[:, cols].astype(f32)
        run = run_ref[h]
        for b in range(q_ref.shape[0] // BLOCK):
            rows = slice(b * BLOCK, (b + 1) * BLOCK)
            q, k, v = q_ref[rows, cols], k_ref[rows, cols], v_ref[rows, cols]
            scores = keep_causal(mm(q, k, 1, 1))
            state = run.astype(bf16)
            attended = mm(scores, v, 1, 0) + mm(q, state, 1, 0)
            run = run + mm(k, v, 0, 0)
            inverse = lax.rsqrt(jnp.mean(attended * attended, axis=-1, keepdims=True) + epsilon)
            row_ref[rows, cols] = (attended * inverse * gain).astype(bf16)
            att_ref[rows, cols] = attended
            s_ref[rows, cols] = scores
            st_ref[rows, cols] = state
        run_ref[h] = run

    owner = step ^ me_ref[0]
    for dist, n_ref in enumerate(n_refs):

        @pl.when(owner == dist)
        def _():
            n_ref[...] = row_ref[...]


def forward(me, query, key, value, gain, before, chunk, cols, nhead):
    tokens, width = query.shape
    tile = tokens // nhead
    heads = cols // HDIM
    spec = pl.BlockSpec((tile, cols), lambda i, m: (i, chunk))
    local = pl.BlockSpec((tile, cols), lambda i, m: (i, 0))
    whole = pl.BlockSpec((tile, cols), lambda i, m: (0, 0))
    outs = pl.pallas_call(
        functools.partial(forward_kernel, nhead),
        grid_spec=pltpu.PrefetchScalarGridSpec(
            num_scalar_prefetch=1,
            grid=(nhead,),
            in_specs=[
                spec,
                spec,
                spec,
                pl.BlockSpec((1, cols), lambda i, m: (0, chunk)),
                pl.BlockSpec((heads, HDIM, HDIM), lambda i, m: (chunk, 0, 0)),
            ],
            out_specs=[whole] * nhead + [local] * 3,
            scratch_shapes=[pltpu.VMEM((heads, HDIM, HDIM), f32), pltpu.VMEM((tile, cols), bf16)],
        ),
        out_shape=[jax.ShapeDtypeStruct((tile, cols), bf16)] * nhead
        + [jax.ShapeDtypeStruct((tokens, cols), kind) for kind in (f32, bf16, bf16)],
        compiler_params=params(32),
        name="forward",
    )(me, query, key, value, gain, before)
    return outs[:nhead], outs[nhead:]


def backward_kernel(nhead, aliased, me_ref, *refs):
    p_refs = refs[:nhead]
    q_ref, k_ref, v_ref, gain_ref, att_ref, st_ref = refs[nhead : nhead + 6]
    gq_ref, g_ref, gs_ref, tot_ref, row_ref = refs[nhead + 6 + aliased :]
    step = pl.program_id(0)
    heads = tot_ref.shape[0]

    @pl.when(step == 0)
    def _():
        tot_ref[...] = jnp.zeros_like(tot_ref)

    for dist, p_ref in enumerate(p_refs):

        @pl.when(step == dist)
        def _():
            row_ref[...] = p_ref[...]

    for h in range(heads):
        cols = slice(h * HDIM, (h + 1) * HDIM)
        gain = gain_ref[:, cols].astype(f32)
        total = tot_ref[h]
        for b in range(q_ref.shape[0] // BLOCK):
            rows = slice(b * BLOCK, (b + 1) * BLOCK)
            q, k, v = q_ref[rows, cols], k_ref[rows, cols], v_ref[rows, cols]
            attended = att_ref[rows, cols]
            inverse = lax.rsqrt(jnp.mean(attended * attended, axis=-1, keepdims=True) + epsilon)
            unit = attended * inverse
            grad_unit = row_ref[rows, cols].astype(f32) * gain
            along = jnp.mean(grad_unit * unit, axis=-1, keepdims=True)
            g = (inverse * (grad_unit - unit * along)).astype(bf16)
            grad_scores = keep_causal(mm(g, v, 1, 1))
            grad_q = mm(grad_scores, k, 1, 0) + mm(g, st_ref[rows, cols], 1, 1)
            total = total + mm(q, g, 0, 0)
            gq_ref[rows, cols] = grad_q.astype(bf16)
            g_ref[rows, cols] = g
            gs_ref[rows, cols] = grad_scores
        tot_ref[h] = total


def backward(me, pieces, query, key, value, gain, attended, states, into, chunk, cols, nhead):
    tokens, width = query.shape
    tile = tokens // nhead
    heads = cols // HDIM
    spec = pl.BlockSpec((tile, cols), lambda i, m: (i ^ m[0], chunk))
    local = pl.BlockSpec((tile, cols), lambda i, m: (i ^ m[0], 0))
    whole = pl.BlockSpec((tile, cols), lambda i, m: (0, 0))
    in_specs = (
        [whole] * nhead
        + [spec] * 3
        + [pl.BlockSpec((1, cols), lambda i, m: (0, chunk)), local, local]
    )
    extra = [] if into is None else [into]
    return pl.pallas_call(
        functools.partial(backward_kernel, nhead, len(extra)),
        grid_spec=pltpu.PrefetchScalarGridSpec(
            num_scalar_prefetch=1,
            grid=(nhead,),
            in_specs=in_specs + [pl.BlockSpec(memory_space=pl.ANY)] * len(extra),
            out_specs=[
                spec,
                local,
                local,
                pl.BlockSpec((heads, HDIM, HDIM), lambda i, m: (0, 0, 0)),
            ],
            scratch_shapes=[pltpu.VMEM((tile, cols), bf16)],
        ),
        out_shape=[
            jax.ShapeDtypeStruct((tokens, width), bf16),
            jax.ShapeDtypeStruct((tokens, cols), bf16),
            jax.ShapeDtypeStruct((tokens, cols), bf16),
            jax.ShapeDtypeStruct((heads, HDIM, HDIM), f32),
        ],
        input_output_aliases={1 + len(in_specs): 0} if extra else {},
        compiler_params=params(32),
        name="backward",
    )(me, *pieces, query, key, value, gain, attended, states, *extra)


def later_kernel(aliased, q_ref, k_ref, v_ref, g_ref, s_ref, gs_ref, after_ref, *refs):
    gk_ref, gv_ref, run_ref = refs[aliased:]
    heads = after_ref.shape[0]

    @pl.when(pl.program_id(0) == 0)
    def _():
        run_ref[...] = after_ref[...]

    for h in range(heads):
        cols = slice(h * HDIM, (h + 1) * HDIM)
        run = run_ref[h]
        for b in reversed(range(q_ref.shape[0] // BLOCK)):
            rows = slice(b * BLOCK, (b + 1) * BLOCK)
            q, k, v, g = q_ref[rows, cols], k_ref[rows, cols], v_ref[rows, cols], g_ref[rows, cols]
            later = run.astype(bf16)
            grad_k = mm(gs_ref[rows, cols], q, 0, 0) + mm(v, later, 1, 1)
            grad_v = mm(s_ref[rows, cols], g, 0, 0) + mm(k, later, 1, 0)
            run = run + mm(q, g, 0, 0)
            gk_ref[rows, cols] = grad_k.astype(bf16)
            gv_ref[rows, cols] = grad_v.astype(bf16)
        run_ref[h] = run


def later_grads(query, key, value, g, scores, grad_scores, after, into, chunk, cols, tile):
    tokens, width = query.shape
    heads = cols // HDIM
    steps = tokens // tile
    spec = pl.BlockSpec((tile, cols), lambda i: (steps - 1 - i, chunk))
    local = pl.BlockSpec((tile, cols), lambda i: (steps - 1 - i, 0))
    extra = [] if into is None else list(into)
    return pl.pallas_call(
        functools.partial(later_kernel, len(extra)),
        grid=(steps,),
        in_specs=[spec] * 3
        + [local] * 3
        + [pl.BlockSpec((heads, HDIM, HDIM), lambda i: (0, 0, 0))]
        + [pl.BlockSpec(memory_space=pl.ANY)] * len(extra),
        out_specs=[spec, spec],
        scratch_shapes=[pltpu.VMEM((heads, HDIM, HDIM), f32)],
        out_shape=[jax.ShapeDtypeStruct((tokens, width), bf16)] * 2,
        input_output_aliases={7: 0, 8: 1} if extra else {},
        compiler_params=params(32),
        name="later_grads",
    )(query, key, value, g, scores, grad_scores, after, *extra)


def project_kernel(n, with_acc, me_ref, *refs):
    x_refs, w_refs = refs[:n], refs[n : 2 * n]
    o_ref = refs[-1]
    total = refs[2 * n][...] if with_acc else None
    for x_ref, w_ref in zip(x_refs, w_refs):
        part = mm(x_ref[...], w_ref[...], 1, 0)
        total = part if total is None else total + part
    o_ref[...] = total.astype(o_ref.dtype)


def project(me, pieces, xs, w_out, acc, chunks, kind):
    rows, cols = xs[0].shape
    model = w_out.shape[1]
    tile = min(512, model)
    n = len(pieces)

    def w_spec(dist, chunk):
        return pl.BlockSpec((cols, tile), lambda j, m: ((m[0] ^ dist) * chunks + chunk, j))

    wide = pl.BlockSpec((rows, tile), lambda j, m: (0, j))
    extra = [] if acc is None else [acc]
    return pl.pallas_call(
        functools.partial(project_kernel, n, len(extra)),
        grid_spec=pltpu.PrefetchScalarGridSpec(
            num_scalar_prefetch=1,
            grid=(model // tile,),
            in_specs=[pl.BlockSpec((rows, cols), lambda j, m: (0, 0))] * n
            + [w_spec(*piece) for piece in pieces]
            + [wide] * len(extra),
            out_specs=wide,
        ),
        out_shape=jax.ShapeDtypeStruct((rows, model), kind),
        compiler_params=params(32),
        name="project",
    )(me, *xs, *([w_out] * n), *extra)


def on_device(nctx, nhead, query, key, value, gain, w_out, d_out):
    tokens, width = query.shape
    local_heads = width // HDIM
    chunks = 2 if local_heads % 2 == 0 else 1
    cols = width // chunks
    me = lax.axis_index("head").astype(jnp.int32).reshape(1)
    place = lax.axis_index("ctx")
    gain = gain.reshape(1, width)

    def swap(array, dist):
        if dist == 0:
            return array
        return lax.ppermute(array, "head", [(i, i ^ dist) for i in range(nhead)])

    def others(total, later):
        outside = jnp.zeros_like(total)
        dist = 1
        while dist < nctx:
            got = lax.ppermute(
                total.astype(bf16), "ctx", [(i, i ^ dist) for i in range(nctx)]
            ).astype(f32)
            wanted = ((place & dist) == 0) == later
            outside = outside + jnp.where(wanted, got, 0.0)
            total = total + got
            dist *= 2
        return outside

    far = [d for d in range(nhead - 1, 0, -1) if d > 1] or []
    near = [d for d in range(nhead) if d <= 1]
    sent = {}
    for c in range(chunks):
        if far:
            pieces = [(d, c) for d in far]
            sent.update(zip(pieces, grad_rows(me, d_out, w_out, pieces, chunks, cols)))
    pieces = [(d, c) for d in near for c in range(chunks)]
    sent.update(zip(pieces, grad_rows(me, d_out, w_out, pieces, chunks, cols)))
    got = {(d, c): swap(sent[d, c], d) for c in range(chunks) for d in reversed(range(nhead))}

    before = others(total_state(key, value), False)

    kept, normed = [], {}
    for c in range(chunks):
        parts, saved = forward(me, query, key, value, gain, before, c, cols, nhead)
        kept.append(saved)
        for d in reversed(range(nhead)):
            normed[d, c] = swap(parts[d], d)

    grad_query, carried = None, []
    for c in range(chunks):
        attended, scores, states = kept[c]
        grad_query, g, grad_scores, total = backward(
            me,
            [got[d, c] for d in range(nhead)],
            query,
            key,
            value,
            gain,
            attended,
            states,
            grad_query,
            c,
            cols,
            nhead,
        )
        carried.append((g, scores, grad_scores, others(total, True)))
    grads = None
    for c in range(chunks):
        grads = later_grads(
            query, key, value, *carried[c], grads, c, cols, tokens // nhead
        )

    last = [(d, chunks - 1) for d in far]
    first = [p for p in normed if p not in last]
    acc = project(
        me, first, [normed[p] for p in first], w_out, None, chunks, f32 if last else bf16
    )
    if last:
        acc = project(me, last, [normed[p] for p in last], w_out, acc, chunks, bf16)
    return acc, grad_query, grads[0], grads[1]


def solution(mesh):
    nctx, nhead = mesh.shape["ctx"], mesh.shape["head"]
    return jax.shard_map(
        functools.partial(on_device, nctx, nhead),
        mesh=mesh,
        in_specs=(
            P("ctx", "head"),
            P("ctx", "head"),
            P("ctx", "head"),
            P("head"),
            P(),
            P(("ctx", "head"), None),
        ),
        out_specs=(P(("ctx", "head"), None), P("ctx", "head"), P("ctx", "head"), P("ctx", "head")),
        check_vma=False,
    )
```

```python
import functools

import jax
import jax.numpy as jnp
from jax import lax
from jax.experimental import pallas as pl
from jax.experimental.pallas import tpu as pltpu
from jax.sharding import PartitionSpec as P

HDIM = 128
BLOCK = 128
epsilon = 1e-06
f32 = jnp.float32
bf16 = jnp.bfloat16
VMEM_LIMIT = 16 << 20


def mm(a, b, ca, cb):
    return lax.dot_general(a, b, (((ca,), (cb,)), ((), ())), preferred_element_type=f32)


def both(a0, a1, b0, b1):
    return mm(jnp.concatenate([a0, a1], 1), jnp.concatenate([b0, b1], 0), 1, 0)


def causal_mask():
    row = lax.broadcasted_iota(jnp.int32, (BLOCK, BLOCK), 0)
    col = lax.broadcasted_iota(jnp.int32, (BLOCK, BLOCK), 1)
    return col <= row


def masked(mask, scores):
    return jnp.where(mask, scores, 0.0).astype(bf16)


def pairs(tile, heads, order=list):
    return [
        (h, (slice(b * BLOCK, (b + 1) * BLOCK), slice(h * HDIM, (h + 1) * HDIM)))
        for b in order(range(tile // BLOCK))
        for h in range(heads)
    ]


def backwards(blocks):
    return list(reversed(blocks))


class Copies:
    def __init__(self, sems):
        self.sems, self.used = sems, 0

    def start(self, src, dst):
        copy = pltpu.make_async_copy(src, dst, self.sems.at[self.used])
        self.used += 1
        copy.start()
        return copy


def span(index, size):
    return pl.ds(pl.multiple_of(index * size, size), size)


def run_kernel(body, args, outs, scratch=(), ncopies=0, name=None, into=None, sent=0):
    here, anywhere = pl.BlockSpec(memory_space=pltpu.VMEM), pl.BlockSpec(memory_space=pl.ANY)
    into = list(into or [])
    return pl.pallas_call(
        body,
        in_specs=[here] * len(args) + [anywhere] * len(into),
        out_specs=[anywhere] * sent + [here] * (len(outs) - sent),
        out_shape=[jax.ShapeDtypeStruct(*out) for out in outs],
        scratch_shapes=[pltpu.VMEM(*s) for s in scratch]
        + ([pltpu.SemaphoreType.DMA((ncopies,))] if ncopies else []),
        input_output_aliases={len(args) + i: i for i in range(len(into))},
        compiler_params=pltpu.CompilerParams(vmem_limit_bytes=VMEM_LIMIT),
        name=name,
    )(*args, *into)


def grad_rows(d_out, w_out, pieces, chunks, cols):
    rows = d_out.shape[0]

    def body(d, w, *outs):
        me = lax.axis_index("head")
        for (dist, c), out in zip(pieces, outs):
            piece = span((me ^ dist) * chunks + c, cols)
            out[...] = mm(d[...], w[piece], 1, 1).astype(bf16)

    return run_kernel(
        body, (d_out, w_out), [((rows, cols), bf16)] * len(pieces), name="grad_rows"
    )


def total_state(key, value):
    heads = key.shape[1] // HDIM
    shape = (heads, HDIM, HDIM)

    def body(k, v, o, ob):
        for h in range(heads):
            cols = slice(h * HDIM, (h + 1) * HDIM)
            total = mm(k[:, cols], v[:, cols], 0, 0)
            o[h] = total
            ob[h] = total.astype(bf16)

    return run_kernel(body, (key, value), [(shape, f32), (shape, bf16)], name="total_state")


def forward(query, key, value, gain, before, chunks, nhead):
    tokens, width = query.shape
    tile, cols = tokens // nhead, width // chunks
    heads = width // HDIM
    n = nhead * chunks

    def body(q, k, v, gain, before, *refs):
        normed, (att, s, st, rows) = refs[:n], refs[n:]
        me = lax.axis_index("head")
        mask = causal_mask()
        run = [before[h] for h in range(heads)]
        for t in range(nhead):
            work = [
                (h, (slice(t * tile + r.start, t * tile + r.stop), c))
                for h, (r, c) in pairs(tile, heads)
            ]
            scores = [masked(mask, mm(q[at], k[at], 1, 1)) for _, at in work]
            for (_, at), x in zip(work, scores):
                s[at] = x
            products = [mm(k[at], v[at], 0, 0) for _, at in work]
            states = []
            for (h, at), product in zip(work, products):
                states.append(run[h].astype(bf16))
                st[at] = states[-1]
                run[h] = run[h] + product
            attended = [both(x, q[at], v[at], y) for (_, at), x, y in zip(work, scores, states)]
            for (_, at), x in zip(work, attended):
                att[at] = x
                inverse = lax.rsqrt(jnp.mean(x * x, axis=-1, keepdims=True) + epsilon)
                rows[at] = (x * inverse * gain[:, at[1]].astype(f32)).astype(bf16)
        for dist in range(nhead):
            part = span(me ^ dist, tile)
            for c in range(chunks):
                normed[dist * chunks + c][...] = rows[part, c * cols : (c + 1) * cols]

    whole = (tokens, width)
    outs = run_kernel(
        body,
        (query, key, value, gain, before),
        [((tile, cols), bf16)] * n + [(whole, f32), (whole, bf16), (whole, bf16)],
        [(whole, bf16)],
        name="forward",
    )
    normed = {(d, c): outs[d * chunks + c] for d in range(nhead) for c in range(chunks)}
    return normed, outs[n:]


def backward(pieces, query, key, value, gain, attended, states, into, chunk, cols):
    tokens, width = query.shape
    nhead = len(pieces)
    tile = tokens // nhead
    heads = cols // HDIM
    shape = (heads, HDIM, HDIM)
    first = chunk * cols

    def body(*refs):
        p, refs = refs[:nhead], refs[nhead:]
        q, k, v, gain, att, st = refs[:6]
        gq_hbm, g, gs, tot, totb, gq, sems = refs[6 + (into is not None) :]
        me = lax.axis_index("head")
        copies = Copies(sems)
        mask = causal_mask()
        stores, sums = [], [0.0] * heads
        for t in range(nhead):
            base = (me ^ t) * tile
            work = [
                (
                    h,
                    (r, c),
                    (span(base // BLOCK + r.start // BLOCK, BLOCK), c),
                    (
                        span(base // BLOCK + r.start // BLOCK, BLOCK),
                        slice(first + c.start, first + c.stop),
                    ),
                )
                for h, (r, c) in pairs(tile, heads)
            ]
            grads = []
            for _, here, near, wide in work:
                x = att[wide]
                inverse = lax.rsqrt(jnp.mean(x * x, axis=-1, keepdims=True) + epsilon)
                unit = x * inverse
                grad_unit = p[t][here].astype(f32) * gain[:, wide[1]].astype(f32)
                along = jnp.mean(grad_unit * unit, axis=-1, keepdims=True)
                grads.append((inverse * (grad_unit - unit * along)).astype(bf16))
                g[near] = grads[-1]
            products = [mm(q[wide], x, 0, 0) for (*_, wide), x in zip(work, grads)]
            for (h, *_), product in zip(work, products):
                sums[h] = sums[h] + product
            grad_scores = [
                masked(mask, mm(x, v[wide], 1, 1)) for (*_, wide), x in zip(work, grads)
            ]
            for (_, _, near, _), x in zip(work, grad_scores):
                gs[near] = x
            for (_, _, near, wide), x, y in zip(work, grad_scores, grads):
                gq[near] = both(x, y, k[wide], st[wide].T).astype(bf16)
            part = span(me ^ t, tile)
            stores.append(copies.start(gq.at[part], gq_hbm.at[part, first : first + cols]))
        for h in range(heads):
            tot[h] = sums[h]
            totb[h] = sums[h].astype(bf16)
        for copy in stores:
            copy.wait()

    local = (tokens, cols)
    return run_kernel(
        body,
        (*pieces, query, key, value, gain, attended, states),
        [((tokens, width), bf16), (local, bf16), (local, bf16), (shape, f32), (shape, bf16)],
        [(local, bf16)],
        nhead,
        "backward",
        into,
        1,
    )


def later_grads(query, key, value, scores, g, grad_scores, after, into, chunk, cols, steps):
    tokens, width = query.shape
    tile, heads = tokens // steps, cols // HDIM
    first = chunk * cols

    def body(*refs):
        q, k, v, s, g, gs, after = refs[:7]
        gk_hbm, gv_hbm, gk, gv, sems = refs[7 + (2 if into else 0) :]
        copies = Copies(sems)
        stores, run = [], [after[h] for h in range(heads)]
        for t in reversed(range(steps)):
            part = pl.ds(t * tile, tile)
            work = []
            for h, (r, c) in pairs(tile, heads, backwards):
                rows = slice(t * tile + r.start, t * tile + r.stop)
                work.append((h, (rows, c), (rows, slice(first + c.start, first + c.stop))))
            products = [mm(q[wide], g[near], 0, 0) for _, near, wide in work]
            laters = []
            for (h, *_), product in zip(work, products):
                laters.append(run[h].astype(bf16))
                run[h] = run[h] + product
            for (_, near, wide), x in zip(work, laters):
                gk[near] = both(gs[near].T, v[wide], q[wide], x.T).astype(bf16)
            mine = slice(first, first + cols)
            stores.append(copies.start(gk.at[part], gk_hbm.at[part, mine]))
            for (_, near, wide), x in zip(work, laters):
                gv[near] = both(s[wide].T, k[wide], g[near], x).astype(bf16)
            stores.append(copies.start(gv.at[part], gv_hbm.at[part, mine]))
        for copy in stores:
            copy.wait()

    local = (tokens, cols)
    return run_kernel(
        body,
        (query, key, value, scores, g, grad_scores, after),
        [((tokens, width), bf16)] * 2,
        [(local, bf16)] * 2,
        2 * steps,
        "later_grads",
        into,
        2,
    )


def project(pieces, xs, w_out, acc, chunks, kind):
    rows, cols = xs[0].shape
    model = w_out.shape[1]
    tile = min(512, model)
    steps, n = model // tile, len(pieces)

    def body(*refs):
        x, w, refs = refs[:n], refs[n], refs[n + 1 :]
        me = lax.axis_index("head")
        deep = jnp.concatenate([ref[...] for ref in x], axis=1)
        rows_of = [span((me ^ dist) * chunks + c, cols) for dist, c in pieces]
        stores = []
        for j in range(steps):
            at = slice(j * tile, (j + 1) * tile)
            total = mm(deep, jnp.concatenate([w[r, at] for r in rows_of], axis=0), 1, 0)
            if acc is not None:
                total = total + refs[0][:, at]
            if kind == f32:
                refs[-1][:, at] = total
            else:
                o_hbm, o, sems = refs[-3:]
                o[:, at] = total.astype(kind)
                stores.append(pltpu.make_async_copy(o.at[:, at], o_hbm.at[:, at], sems.at[j]))
                stores[-1].start()
        for copy in stores:
            copy.wait()

    final = kind == bf16
    return run_kernel(
        body,
        (*xs, w_out) + (() if acc is None else (acc,)),
        [((rows, model), kind)],
        [((rows, model), kind)] if final else [],
        steps if final else 0,
        "project",
        sent=int(final),
    )[0]


def on_device(nctx, nhead, query, key, value, gain, w_out, d_out):
    tokens, width = query.shape
    local_heads = width // HDIM
    chunks = 2 if local_heads % 2 == 0 else 1
    cols = width // chunks
    place = lax.axis_index("ctx")
    gain = gain.reshape(1, width)

    def swap(array, dist):
        if dist == 0:
            return array
        return lax.ppermute(array, "head", [(i, i ^ dist) for i in range(nhead)])

    def others(total, rounded, later):
        outside = jnp.zeros_like(total)
        dist = 1
        while dist < nctx:
            got = lax.ppermute(rounded, "ctx", [(i, i ^ dist) for i in range(nctx)]).astype(f32)
            wanted = ((place & dist) == 0) == later
            outside = outside + jnp.where(wanted, got, 0.0)
            total = total + got
            rounded = total.astype(bf16)
            dist *= 2
        return outside

    far = [d for d in range(nhead - 1, 0, -1) if d > 1]
    near = [d for d in range(nhead) if d <= 1]
    sent = {}
    for c in range(chunks):
        pieces = [(d, c) for d in far]
        if far:
            sent.update(zip(pieces, grad_rows(d_out, w_out, pieces, chunks, cols)))
    pieces = [(d, c) for d in near for c in range(chunks)]
    sent.update(zip(pieces, grad_rows(d_out, w_out, pieces, chunks, cols)))
    got = {(d, c): swap(sent[d, c], d) for c in range(chunks) for d in reversed(range(nhead))}

    before = others(*total_state(key, value), False)

    normed, (attended, scores, states) = forward(query, key, value, gain, before, chunks, nhead)
    normed = {(d, c): swap(normed[d, c], d) for c in range(chunks) for d in reversed(range(nhead))}

    grad_query, carried = None, []
    for c in range(chunks):
        grad_query, g, grad_scores, total, rounded = backward(
            [got[d, c] for d in range(nhead)],
            query,
            key,
            value,
            gain,
            attended,
            states,
            grad_query,
            c,
            cols,
        )
        grad_query = [grad_query]
        carried.append((g, grad_scores, others(total, rounded, True)))
    grads = None
    for c in range(chunks):
        grads = later_grads(query, key, value, scores, *carried[c], grads, c, cols, nhead)

    last = [(d, chunks - 1) for d in far]
    first = [p for p in normed if p not in last]
    out = project(first, [normed[p] for p in first], w_out, None, chunks, f32 if last else bf16)
    if last:
        out = project(last, [normed[p] for p in last], w_out, out, chunks, bf16)
    return out, grad_query[0], grads[0], grads[1]


def solution(mesh):
    nctx, nhead = mesh.shape["ctx"], mesh.shape["head"]
    return jax.shard_map(
        functools.partial(on_device, nctx, nhead),
        mesh=mesh,
        in_specs=(
            P("ctx", "head"),
            P("ctx", "head"),
            P("ctx", "head"),
            P("head"),
            P(),
            P(("ctx", "head"), None),
        ),
        out_specs=(P(("ctx", "head"), None), P("ctx", "head"), P("ctx", "head"), P("ctx", "head")),
        check_vma=False,
    )
```

```python
import functools

import jax
import jax.numpy as jnp
from jax import lax
from jax.experimental import pallas as pl
from jax.experimental.pallas import tpu as pltpu
from jax.sharding import PartitionSpec as P

HDIM = 128
BLOCK = 128
epsilon = 1e-06
f32 = jnp.float32
bf16 = jnp.bfloat16
VMEM_LIMIT = 16 << 20
COST = {'grad_rows': 553680000, 'total_state': 276840000, 'forward': 1349595000, 'backward': 1280385000, 'later_grads': 986242500, 'project': 692100000, 'second_part': 69210000, 'held_back': 103815000}


def mm(a, b, ca, cb):
    return lax.dot_general(a, b, (((ca,), (cb,)), ((), ())), preferred_element_type=f32)


def both(a0, a1, b0, b1):
    return mm(jnp.concatenate([a0, a1], 1), jnp.concatenate([b0, b1], 0), 1, 0)


def causal_mask():
    row = lax.broadcasted_iota(jnp.int32, (BLOCK, BLOCK), 0)
    col = lax.broadcasted_iota(jnp.int32, (BLOCK, BLOCK), 1)
    return col <= row


def masked(mask, scores):
    return jnp.where(mask, scores, 0.0).astype(bf16)


def pairs(tile, heads, order=list):
    return [
        (h, (slice(b * BLOCK, (b + 1) * BLOCK), slice(h * HDIM, (h + 1) * HDIM)))
        for b in order(range(tile // BLOCK))
        for h in range(heads)
    ]


def backwards(blocks):
    return list(reversed(blocks))


class Copies:
    def __init__(self, sems):
        self.sems, self.used = sems, 0

    def start(self, src, dst):
        copy = pltpu.make_async_copy(src, dst, self.sems.at[self.used])
        self.used += 1
        copy.start()
        return copy


def span(index, size):
    return pl.ds(pl.multiple_of(index * size, size), size)


def run_kernel(body, args, outs, scratch=(), ncopies=0, name=None, into=(), sent=0, after=()):
    here, anywhere = pl.BlockSpec(memory_space=pltpu.VMEM), pl.BlockSpec(memory_space=pl.ANY)
    skip = len(after)
    return pl.pallas_call(
        lambda *refs: body(*refs[skip:]),
        in_specs=[anywhere] * skip + [here] * len(args) + [anywhere] * len(into),
        out_specs=[anywhere] * sent + [here] * (len(outs) - sent),
        out_shape=[jax.ShapeDtypeStruct(*out) for out in outs],
        scratch_shapes=[pltpu.VMEM(*s) for s in scratch]
        + ([pltpu.SemaphoreType.DMA((ncopies,))] if ncopies else []),
        input_output_aliases={skip + len(args) + i: i for i in range(len(into))},
        compiler_params=pltpu.CompilerParams(vmem_limit_bytes=VMEM_LIMIT),
        cost_estimate=pl.CostEstimate(flops=COST[name], bytes_accessed=0, transcendentals=0),
        name=name,
    )(*after, *args, *into)


def grad_rows(d_out, w_out, groups, width, chunks, after=(), beside=()):
    rows, cols = d_out.shape[0], width // chunks

    def body(d, w, *outs):
        me, outs = lax.axis_index("head"), outs[len(beside) :]
        for c in range(chunks):
            for group, out in zip(groups, outs[c * len(groups) :]):
                for i, dist in enumerate(group):
                    piece = span((me ^ dist) * chunks + c, cols)
                    out[i] = mm(d[...], w[piece], 1, 1).astype(bf16)

    return run_kernel(
        body,
        (d_out, w_out, *beside),
        [((len(group), rows, cols), bf16) for _ in range(chunks) for group in groups],
        name="grad_rows",
        after=after,
    )


def held_back(array, after):
    def body(array, out):
        out[...] = array[...]

    return run_kernel(body, (array,), [(array.shape, array.dtype)], name="held_back", after=after)[0]


def second_part(got, after):
    def body(got, out):
        out[0] = got[1]

    (out,) = run_kernel(
        body, (got,), [((1,) + got.shape[1:], got.dtype)], name="second_part", after=after
    )
    return out


def total_state(key, value, after):
    heads = key.shape[1] // HDIM
    shape = (heads, HDIM, HDIM)

    def body(k, v, o, ob):
        for h in range(heads):
            cols = slice(h * HDIM, (h + 1) * HDIM)
            total = mm(k[:, cols], v[:, cols], 0, 0)
            o[h] = total
            ob[h] = total.astype(bf16)

    return run_kernel(body, (key, value), [(shape, f32), (shape, bf16)], name="total_state", after=after)


def outside(arrived, later):
    place = lax.axis_index("ctx")
    total = 0.0
    for step, got in enumerate(arrived):
        wanted = (((place >> step) & 1) == 0) == later
        total = total + jnp.where(wanted, got[...].astype(f32), 0.0)
    return total


def forward(query, key, value, gain, arrived, groups, after):
    tokens, width = query.shape
    nhead, n = sum(map(len, groups)), len(groups)
    tile, heads = tokens // nhead, width // HDIM

    def body(q, k, v, gain, *refs):
        before, refs = outside(refs[: len(arrived)], False), refs[len(arrived) :]
        normed, (att, s, st, rows) = refs[:n], refs[n:]
        me = lax.axis_index("head")
        mask = causal_mask()
        run = [before[h] for h in range(heads)]
        for t in range(nhead):
            work = [
                (h, (slice(t * tile + r.start, t * tile + r.stop), c))
                for h, (r, c) in pairs(tile, heads)
            ]
            scores = [masked(mask, mm(q[at], k[at], 1, 1)) for _, at in work]
            for (_, at), x in zip(work, scores):
                s[at] = x
            products = [mm(k[at], v[at], 0, 0) for _, at in work]
            states = []
            for (h, at), product in zip(work, products):
                states.append(run[h].astype(bf16))
                st[at] = states[-1]
                run[h] = run[h] + product
            attended = [both(x, q[at], v[at], y) for (_, at), x, y in zip(work, scores, states)]
            for (_, at), x in zip(work, attended):
                att[at] = x
                inverse = lax.rsqrt(jnp.mean(x * x, axis=-1, keepdims=True) + epsilon)
                rows[at] = (x * inverse * gain[:, at[1]].astype(f32)).astype(bf16)
        for group, out in zip(groups, normed):
            for i, dist in enumerate(group):
                out[i] = rows[span(me ^ dist, tile)]

    whole = (tokens, width)
    outs = run_kernel(
        body,
        (query, key, value, gain, *arrived),
        [((len(group), tile, width), bf16) for group in groups]
        + [(whole, f32), (whole, bf16), (whole, bf16)],
        [(whole, bf16)],
        name="forward",
        after=after,
    )
    return outs[:n], outs[n:]


def backward(pieces, query, key, value, gain, attended, states, into, chunk, cols):
    tokens, width = query.shape
    nhead = len(pieces)
    tile = tokens // nhead
    heads = cols // HDIM
    shape = (heads, HDIM, HDIM)
    first = chunk * cols
    shifts = [first if piece.shape[2] == width else 0 for piece in pieces]

    def body(*refs):
        p, refs = refs[:nhead], refs[nhead:]
        q, k, v, gain, att, st = refs[:6]
        gq_hbm, g, gs, tot, totb, gq, sems = refs[6 + len(into) :]
        me = lax.axis_index("head")
        copies = Copies(sems)
        mask = causal_mask()
        stores, sums = [], [0.0] * heads
        for t in range(nhead):
            base = (me ^ t) * tile
            work = [
                (
                    h,
                    (r, c),
                    (span(base // BLOCK + r.start // BLOCK, BLOCK), c),
                    (
                        span(base // BLOCK + r.start // BLOCK, BLOCK),
                        slice(first + c.start, first + c.stop),
                    ),
                )
                for h, (r, c) in pairs(tile, heads)
            ]
            grads = []
            for _, here, near, wide in work:
                x = att[wide]
                inverse = lax.rsqrt(jnp.mean(x * x, axis=-1, keepdims=True) + epsilon)
                unit = x * inverse
                at = slice(shifts[t] + here[1].start, shifts[t] + here[1].stop)
                grad_unit = p[t][0, here[0], at].astype(f32) * gain[:, wide[1]].astype(f32)
                along = jnp.mean(grad_unit * unit, axis=-1, keepdims=True)
                grads.append((inverse * (grad_unit - unit * along)).astype(bf16))
                g[near] = grads[-1]
            products = [mm(q[wide], x, 0, 0) for (*_, wide), x in zip(work, grads)]
            for (h, *_), product in zip(work, products):
                sums[h] = sums[h] + product
            grad_scores = [
                masked(mask, mm(x, v[wide], 1, 1)) for (*_, wide), x in zip(work, grads)
            ]
            for (_, _, near, _), x in zip(work, grad_scores):
                gs[near] = x
            for (_, _, near, wide), x, y in zip(work, grad_scores, grads):
                gq[near] = both(x, y, k[wide], st[wide].T).astype(bf16)
            part = span(me ^ t, tile)
            stores.append(copies.start(gq.at[part], gq_hbm.at[part, first : first + cols]))
        for h in range(heads):
            tot[h] = sums[h]
            totb[h] = sums[h].astype(bf16)
        for copy in stores:
            copy.wait()

    local = (tokens, cols)
    return run_kernel(
        body,
        (*pieces, query, key, value, gain, attended, states),
        [((tokens, width), bf16), (local, bf16), (local, bf16), (shape, f32), (shape, bf16)],
        [(local, bf16)],
        nhead,
        "backward",
        into,
        1,
    )


def later_grads(query, key, value, scores, g, grad_scores, arrived, into, chunk, cols, steps):
    tokens, width = query.shape
    tile, heads = tokens // steps, cols // HDIM
    first = chunk * cols

    def body(*refs):
        q, k, v, s, g, gs = refs[:6]
        after, refs = outside(refs[6 : 6 + len(arrived)], True), refs[6 + len(arrived) :]
        gk_hbm, gv_hbm, gk, gv, sems = refs[len(into) :]
        copies = Copies(sems)
        stores, run = [], [after[h] for h in range(heads)]
        for t in reversed(range(steps)):
            part = pl.ds(t * tile, tile)
            work = []
            for h, (r, c) in pairs(tile, heads, backwards):
                rows = slice(t * tile + r.start, t * tile + r.stop)
                work.append((h, (rows, c), (rows, slice(first + c.start, first + c.stop))))
            products = [mm(q[wide], g[near], 0, 0) for _, near, wide in work]
            laters = []
            for (h, *_), product in zip(work, products):
                laters.append(run[h].astype(bf16))
                run[h] = run[h] + product
            for (_, near, wide), x in zip(work, laters):
                gk[near] = both(gs[near].T, v[wide], q[wide], x.T).astype(bf16)
            mine = slice(first, first + cols)
            stores.append(copies.start(gk.at[part], gk_hbm.at[part, mine]))
            for (_, near, wide), x in zip(work, laters):
                gv[near] = both(s[wide].T, k[wide], g[near], x).astype(bf16)
            stores.append(copies.start(gv.at[part], gv_hbm.at[part, mine]))
        for copy in stores:
            copy.wait()

    local = (tokens, cols)
    return run_kernel(
        body,
        (query, key, value, scores, g, grad_scores, *arrived),
        [((tokens, width), bf16)] * 2,
        [(local, bf16)] * 2,
        2 * steps,
        "later_grads",
        into,
        2,
    )


def project(dists, xs, w_out, acc, kind, hand_on=False, after=()):
    _, rows, width = xs[0].shape
    model = w_out.shape[1]
    tile = min(512, model)
    steps, n = model // tile, len(dists)
    final = kind == bf16

    def body(*refs):
        x, w, refs = refs[:n], refs[n], refs[n + 1 :]
        acc_ref, refs = (refs[0], refs[1:]) if acc is not None else (None, refs)
        me = lax.axis_index("head")
        if hand_on:
            refs[1][0] = x[0][1]
        deep = jnp.concatenate([ref[0] for ref in x], axis=1)
        rows_of = [span(me ^ dist, width) for dist in dists]
        stores = []
        for j in range(steps):
            at = slice(j * tile, (j + 1) * tile)
            total = mm(deep, jnp.concatenate([w[r, at] for r in rows_of], axis=0), 1, 0)
            if acc is not None:
                total = total + acc_ref[:, at]
            if final:
                o_hbm, o, sems = refs
                o[:, at] = total.astype(kind)
                stores.append(pltpu.make_async_copy(o.at[:, at], o_hbm.at[:, at], sems.at[j]))
                stores[-1].start()
            else:
                refs[0][:, at] = total
        for copy in stores:
            copy.wait()

    outs = run_kernel(
        body,
        (*xs, w_out) + (() if acc is None else (acc,)),
        [((rows, model), kind)] + [((1, rows, width), bf16)] * hand_on,
        [((rows, model), kind)] if final else [],
        steps if final else 0,
        "project",
        sent=int(final),
        after=after,
    )
    return outs if hand_on else outs[0]


def on_device(nctx, nhead, query, key, value, gain, w_out, d_out):
    tokens, width = query.shape
    local_heads = width // HDIM
    chunks = 2 if local_heads % 2 == 0 else 1
    cols = width // chunks
    gain = gain.reshape(1, width)

    def swap(array, dist):
        return lax.ppermute(array, "head", [(i, i ^ dist) for i in range(nhead)])

    pairs_of = [(d, d + 1) for d in range(2, nhead, 2)]
    near = [(d,) for d in range(min(nhead, 2))]
    groups = pairs_of + near

    def scan(total, rounded):
        arrived = []
        dist = 1
        while dist < nctx:
            arrived.append(lax.ppermute(rounded, "ctx", [(i, i ^ dist) for i in range(nctx)]))
            dist *= 2
            if dist < nctx:
                total = total + arrived[-1].astype(f32)
                rounded = total.astype(bf16)
        return arrived

    pieces = [{} for _ in range(chunks)]
    sent = grad_rows(d_out, w_out, pairs_of, width, chunks) if pairs_of else []

    def send_far(c, after):
        for i, group in enumerate(pairs_of):
            out = sent[c * len(pairs_of) + i]
            pieces[c][group[0]] = swap(held_back(out, after) if after else out, group[0])

    def hand_on(c, after):
        for group in pairs_of:
            pieces[c][group[1]] = swap(second_part(pieces[c][group[0]], after), 1)

    send_far(0, ())
    total, rounded = total_state(key, value, sent)
    arrived = scan(total, rounded)
    mine = []
    for group, out in zip(near, grad_rows(d_out, w_out, near, width, 1, (rounded,), (query, value))):
        mine.append(swap(out, group[0]) if group[0] else out)
        for c in range(chunks):
            pieces[c][group[0]] = mine[-1]
    for c in range(1, chunks):
        send_far(c, [pieces[c - 1][group[0]] for group in pairs_of] + arrived[1:2] + mine[:1])
    normed, (attended, scores, states) = forward(
        query, key, value, gain, arrived, groups, mine[:1]
    )
    normed = {group: swap(x, group[0]) if group[0] else x for group, x in zip(groups, normed)}
    out = project(
        [d for d, in near],
        [normed[group] for group in near],
        w_out,
        None,
        f32 if pairs_of else bf16,
    )

    grad_query, carried, afters = [], [], []
    for c in range(chunks):
        hand_on(c, [attended])
        query_part, g, grad_scores, total, rounded = backward(
            [pieces[c][d] for d in range(nhead)],
            query,
            key,
            value,
            gain,
            attended,
            states,
            grad_query,
            c,
            cols,
        )
        grad_query = [query_part]
        afters.append(scan(total, rounded))
        carried.append((g, grad_scores))
    grads = []
    for c in range(chunks):
        grads = later_grads(
            query, key, value, scores, *carried[c], afters[c], grads, c, cols, nhead
        )

    for group in pairs_of:
        out, second = project(group[:1], [normed[group]], w_out, out, f32, True, [a[-1] for a in afters])
        out = project(
            group[1:], [swap(second, 1)], w_out, out, bf16 if group == pairs_of[-1] else f32
        )
    return out, grad_query[0], *grads


def solution(mesh):
    nctx, nhead = mesh.shape["ctx"], mesh.shape["head"]
    return jax.shard_map(
        functools.partial(on_device, nctx, nhead),
        mesh=mesh,
        in_specs=(
            P("ctx", "head"),
            P("ctx", "head"),
            P("ctx", "head"),
            P("head"),
            P(),
            P(("ctx", "head"), None),
        ),
        out_specs=(P(("ctx", "head"), None), P("ctx", "head"), P("ctx", "head"), P("ctx", "head")),
        check_vma=False,
    )
```

```python
import functools

import jax
import jax.numpy as jnp
from jax import lax
from jax.experimental import pallas as pl
from jax.experimental.pallas import tpu as pltpu
from jax.sharding import PartitionSpec as P

HDIM = 128
BLOCK = 128
epsilon = 1e-06
f32 = jnp.float32
bf16 = jnp.bfloat16
VMEM_LIMIT = 16 << 20
COST = {'grad_rows': 553680000, 'total_state': 276840000, 'forward': 1349595000, 'backward': 1280385000, 'later_grads': 986242500, 'project': 692100000, 'second_part': 69210000, 'held_back': 103815000}


def mm(a, b, ca, cb):
    return lax.dot_general(a, b, (((ca,), (cb,)), ((), ())), preferred_element_type=f32)


def both(a0, a1, b0, b1):
    return mm(jnp.concatenate([a0, a1], 1), jnp.concatenate([b0, b1], 0), 1, 0)


def causal_mask():
    row = lax.broadcasted_iota(jnp.int32, (BLOCK, BLOCK), 0)
    col = lax.broadcasted_iota(jnp.int32, (BLOCK, BLOCK), 1)
    return col <= row


def masked(mask, scores):
    return jnp.where(mask, scores, 0.0).astype(bf16)


def pairs(tile, heads, order=list):
    return [
        (h, (slice(b * BLOCK, (b + 1) * BLOCK), slice(h * HDIM, (h + 1) * HDIM)))
        for b in order(range(tile // BLOCK))
        for h in range(heads)
    ]


def backwards(blocks):
    return list(reversed(blocks))


class Copies:
    def __init__(self, sems):
        self.sems, self.used = sems, 0

    def start(self, src, dst):
        copy = pltpu.make_async_copy(src, dst, self.sems.at[self.used])
        self.used += 1
        copy.start()
        return copy


def span(index, size):
    return pl.ds(pl.multiple_of(index * size, size), size)


def run_kernel(body, args, outs, scratch=(), ncopies=0, name=None, into=(), sent=0, after=()):
    here, anywhere = pl.BlockSpec(memory_space=pltpu.VMEM), pl.BlockSpec(memory_space=pl.ANY)
    skip = len(after)
    return pl.pallas_call(
        lambda *refs: body(*refs[skip:]),
        in_specs=[anywhere] * skip + [here] * len(args) + [anywhere] * len(into),
        out_specs=[anywhere] * sent + [here] * (len(outs) - sent),
        out_shape=[jax.ShapeDtypeStruct(*out) for out in outs],
        scratch_shapes=[pltpu.VMEM(*s) for s in scratch]
        + ([pltpu.SemaphoreType.DMA((ncopies,))] if ncopies else []),
        input_output_aliases={skip + len(args) + i: i for i in range(len(into))},
        compiler_params=pltpu.CompilerParams(vmem_limit_bytes=VMEM_LIMIT),
        cost_estimate=pl.CostEstimate(flops=COST[name], bytes_accessed=0, transcendentals=0),
        name=name,
    )(*after, *args, *into)


def grad_rows(d_out, w_out, groups, width, chunks, after=(), beside=()):
    rows, cols = d_out.shape[0], width // chunks

    def body(d, w, *outs):
        me, outs = lax.axis_index("head"), outs[len(beside) :]
        for c in range(chunks):
            for group, out in zip(groups, outs[c * len(groups) :]):
                for i, dist in enumerate(group):
                    piece = span((me ^ dist) * chunks + c, cols)
                    out[i] = mm(d[...], w[piece], 1, 1).astype(bf16)

    return run_kernel(
        body,
        (d_out, w_out, *beside),
        [((len(group), rows, cols), bf16) for _ in range(chunks) for group in groups],
        name="grad_rows",
        after=after,
    )


def held_back(array, after):
    def body(array, out):
        out[...] = array[...]

    return run_kernel(body, (array,), [(array.shape, array.dtype)], name="held_back", after=after)[0]


def second_part(got, after):
    def body(got, out):
        out[0] = got[1]

    (out,) = run_kernel(
        body, (got,), [((1,) + got.shape[1:], got.dtype)], name="second_part", after=after
    )
    return out


def total_state(key, value, after):
    heads = key.shape[1] // HDIM
    shape = (heads, HDIM, HDIM)

    def body(k, v, o, ob):
        for h in range(heads):
            cols = slice(h * HDIM, (h + 1) * HDIM)
            total = mm(k[:, cols], v[:, cols], 0, 0)
            o[h] = total
            ob[h] = total.astype(bf16)

    return run_kernel(body, (key, value), [(shape, f32), (shape, bf16)], name="total_state", after=after)


def outside(arrived, later):
    place = lax.axis_index("ctx")
    total = 0.0
    for step, got in enumerate(arrived):
        wanted = (((place >> step) & 1) == 0) == later
        total = total + jnp.where(wanted, got[...].astype(f32), 0.0)
    return total


def forward(query, key, value, gain, arrived, groups, after):
    tokens, width = query.shape
    nhead, n = sum(map(len, groups)), len(groups)
    tile, heads = tokens // nhead, width // HDIM

    def body(q, k, v, gain, *refs):
        before, refs = outside(refs[: len(arrived)], False), refs[len(arrived) :]
        normed, (att, s, st, rows) = refs[:n], refs[n:]
        me = lax.axis_index("head")
        mask = causal_mask()
        run = [before[h] for h in range(heads)]
        for t in range(nhead):
            work = [
                (h, (slice(t * tile + r.start, t * tile + r.stop), c))
                for h, (r, c) in pairs(tile, heads)
            ]
            scores = [masked(mask, mm(q[at], k[at], 1, 1)) for _, at in work]
            for (_, at), x in zip(work, scores):
                s[at] = x
            products = [mm(k[at], v[at], 0, 0) for _, at in work]
            states = []
            for (h, at), product in zip(work, products):
                states.append(run[h].astype(bf16))
                st[at] = states[-1]
                run[h] = run[h] + product
            attended = [both(x, q[at], v[at], y) for (_, at), x, y in zip(work, scores, states)]
            for (_, at), x in zip(work, attended):
                att[at] = x
                inverse = lax.rsqrt(jnp.mean(x * x, axis=-1, keepdims=True) + epsilon)
                rows[at] = (x * inverse * gain[:, at[1]].astype(f32)).astype(bf16)
        for group, out in zip(groups, normed):
            for i, dist in enumerate(group):
                out[i] = rows[span(me ^ dist, tile)]

    whole = (tokens, width)
    outs = run_kernel(
        body,
        (query, key, value, gain, *arrived),
        [((len(group), tile, width), bf16) for group in groups]
        + [(whole, f32), (whole, bf16), (whole, bf16)],
        [(whole, bf16)],
        name="forward",
        after=after,
    )
    return outs[:n], outs[n:]


def backward(pieces, query, key, value, gain, attended, states, into, chunk, cols):
    tokens, width = query.shape
    nhead = len(pieces)
    tile = tokens // nhead
    heads = cols // HDIM
    shape = (heads, HDIM, HDIM)
    first = chunk * cols
    shifts = [first if piece.shape[2] == width else 0 for piece in pieces]

    def body(*refs):
        p, refs = refs[:nhead], refs[nhead:]
        q, k, v, gain, att, st = refs[:6]
        gq_hbm, g, gs, tot, totb, gq, sems = refs[6 + len(into) :]
        me = lax.axis_index("head")
        copies = Copies(sems)
        mask = causal_mask()
        stores, sums = [], [0.0] * heads
        for t in range(nhead):
            base = (me ^ t) * tile
            work = [
                (
                    h,
                    (r, c),
                    (span(base // BLOCK + r.start // BLOCK, BLOCK), c),
                    (
                        span(base // BLOCK + r.start // BLOCK, BLOCK),
                        slice(first + c.start, first + c.stop),
                    ),
                )
                for h, (r, c) in pairs(tile, heads)
            ]
            grads = []
            for _, here, near, wide in work:
                x = att[wide]
                inverse = lax.rsqrt(jnp.mean(x * x, axis=-1, keepdims=True) + epsilon)
                unit = x * inverse
                at = slice(shifts[t] + here[1].start, shifts[t] + here[1].stop)
                grad_unit = p[t][0, here[0], at].astype(f32) * gain[:, wide[1]].astype(f32)
                along = jnp.mean(grad_unit * unit, axis=-1, keepdims=True)
                grads.append((inverse * (grad_unit - unit * along)).astype(bf16))
                g[near] = grads[-1]
            products = [mm(q[wide], x, 0, 0) for (*_, wide), x in zip(work, grads)]
            for (h, *_), product in zip(work, products):
                sums[h] = sums[h] + product
            grad_scores = [
                masked(mask, mm(x, v[wide], 1, 1)) for (*_, wide), x in zip(work, grads)
            ]
            for (_, _, near, _), x in zip(work, grad_scores):
                gs[near] = x
            for (_, _, near, wide), x, y in zip(work, grad_scores, grads):
                gq[near] = both(x, y, k[wide], st[wide].T).astype(bf16)
            part = span(me ^ t, tile)
            stores.append(copies.start(gq.at[part], gq_hbm.at[part, first : first + cols]))
        for h in range(heads):
            tot[h] = sums[h]
            totb[h] = sums[h].astype(bf16)
        for copy in stores:
            copy.wait()

    local = (tokens, cols)
    return run_kernel(
        body,
        (*pieces, query, key, value, gain, attended, states),
        [((tokens, width), bf16), (local, bf16), (local, bf16), (shape, f32), (shape, bf16)],
        [(local, bf16)],
        nhead,
        "backward",
        into,
        1,
    )


def later_grads(query, key, value, scores, g, grad_scores, arrived, into, chunk, cols, steps):
    tokens, width = query.shape
    tile, heads = tokens // steps, cols // HDIM
    first = chunk * cols

    def body(*refs):
        q, k, v, s, g, gs = refs[:6]
        after, refs = outside(refs[6 : 6 + len(arrived)], True), refs[6 + len(arrived) :]
        gk_hbm, gv_hbm, token, gk, gv, sems = refs[len(into) :]
        token[...] = jnp.zeros_like(token)
        copies = Copies(sems)
        stores, run = [], [after[h] for h in range(heads)]
        for t in reversed(range(steps)):
            part = pl.ds(t * tile, tile)
            work = []
            for h, (r, c) in pairs(tile, heads, backwards):
                rows = slice(t * tile + r.start, t * tile + r.stop)
                work.append((h, (rows, c), (rows, slice(first + c.start, first + c.stop))))
            products = [mm(q[wide], g[near], 0, 0) for _, near, wide in work]
            laters = []
            for (h, *_), product in zip(work, products):
                laters.append(run[h].astype(bf16))
                run[h] = run[h] + product
            for (_, near, wide), x in zip(work, laters):
                gk[near] = both(gs[near].T, v[wide], q[wide], x.T).astype(bf16)
            mine = slice(first, first + cols)
            stores.append(copies.start(gk.at[part], gk_hbm.at[part, mine]))
            for (_, near, wide), x in zip(work, laters):
                gv[near] = both(s[wide].T, k[wide], g[near], x).astype(bf16)
            stores.append(copies.start(gv.at[part], gv_hbm.at[part, mine]))
        for copy in stores:
            copy.wait()

    local = (tokens, cols)
    return run_kernel(
        body,
        (query, key, value, scores, g, grad_scores, *arrived),
        [((tokens, width), bf16)] * 2 + [((8, HDIM), f32)],
        [(local, bf16)] * 2,
        2 * steps,
        "later_grads",
        into,
        2,
    )


def project(dists, xs, w_out, acc, kind, hand_on=False, after=()):
    _, rows, width = xs[0].shape
    model = w_out.shape[1]
    tile = min(512, model)
    steps, n = model // tile, len(dists)
    final = kind == bf16

    def body(*refs):
        x, w, refs = refs[:n], refs[n], refs[n + 1 :]
        acc_ref, refs = (refs[0], refs[1:]) if acc is not None else (None, refs)
        me = lax.axis_index("head")
        if hand_on:
            refs[1][0] = x[0][1]
        deep = jnp.concatenate([ref[0] for ref in x], axis=1)
        rows_of = [span(me ^ dist, width) for dist in dists]
        stores = []
        for j in range(steps):
            at = slice(j * tile, (j + 1) * tile)
            total = mm(deep, jnp.concatenate([w[r, at] for r in rows_of], axis=0), 1, 0)
            if acc is not None:
                total = total + acc_ref[:, at]
            if final:
                o_hbm, o, sems = refs
                o[:, at] = total.astype(kind)
                stores.append(pltpu.make_async_copy(o.at[:, at], o_hbm.at[:, at], sems.at[j]))
                stores[-1].start()
            else:
                refs[0][:, at] = total
        for copy in stores:
            copy.wait()

    outs = run_kernel(
        body,
        (*xs, w_out) + (() if acc is None else (acc,)),
        [((rows, model), kind)] + [((1, rows, width), bf16)] * hand_on,
        [((rows, model), kind)] if final else [],
        steps if final else 0,
        "project",
        sent=int(final),
        after=after,
    )
    return outs if hand_on else outs[0]


def on_device(nctx, nhead, query, key, value, gain, w_out, d_out):
    tokens, width = query.shape
    local_heads = width // HDIM
    chunks = 2 if local_heads % 2 == 0 else 1
    cols = width // chunks
    gain = gain.reshape(1, width)

    def swap(array, dist):
        return lax.ppermute(array, "head", [(i, i ^ dist) for i in range(nhead)])

    pairs_of = [(d, d + 1) for d in range(2, nhead, 2)]
    near = [(d,) for d in range(min(nhead, 2))]
    groups = pairs_of + near

    def scan(total, rounded):
        arrived = []
        dist = 1
        while dist < nctx:
            arrived.append(lax.ppermute(rounded, "ctx", [(i, i ^ dist) for i in range(nctx)]))
            dist *= 2
            if dist < nctx:
                total = total + arrived[-1].astype(f32)
                rounded = total.astype(bf16)
        return arrived

    pieces = [{} for _ in range(chunks)]
    sent = grad_rows(d_out, w_out, pairs_of, width, chunks) if pairs_of else []

    def send_far(c, after):
        for i, group in enumerate(pairs_of):
            out = sent[c * len(pairs_of) + i]
            pieces[c][group[0]] = swap(held_back(out, after) if after else out, group[0])

    def hand_on(c, after):
        for group in pairs_of:
            pieces[c][group[1]] = swap(second_part(pieces[c][group[0]], after), 1)

    send_far(0, ())
    total, rounded = total_state(key, value, sent)
    arrived = scan(total, rounded)
    mine = []
    for group, out in zip(near, grad_rows(d_out, w_out, near, width, 1, (rounded,), (query, value))):
        mine.append(swap(out, group[0]) if group[0] else out)
        for c in range(chunks):
            pieces[c][group[0]] = mine[-1]
    for c in range(1, chunks):
        send_far(c, [pieces[c - 1][group[0]] for group in pairs_of] + arrived[1:2] + mine[:1])
    normed, (attended, scores, states) = forward(
        query, key, value, gain, arrived, groups, mine[:1]
    )
    normed = {group: swap(x, group[0]) if group[0] else x for group, x in zip(groups, normed)}
    out = project(
        [d for d, in near],
        [normed[group] for group in near],
        w_out,
        None,
        f32 if pairs_of else bf16,
    )

    grad_query, carried, afters = [], [], []
    for c in range(chunks):
        hand_on(c, [attended])
        query_part, g, grad_scores, total, rounded = backward(
            [pieces[c][d] for d in range(nhead)],
            query,
            key,
            value,
            gain,
            attended,
            states,
            grad_query,
            c,
            cols,
        )
        grad_query = [query_part]
        afters.append(scan(total, rounded))
        carried.append((g, grad_scores))
    grads, tokens_out = [], []
    for c in range(chunks):
        *grads, token = later_grads(
            query, key, value, scores, *carried[c], afters[c], grads, c, cols, nhead
        )
        tokens_out.append(token)

    for group in pairs_of:
        out, second = project(group[:1], [normed[group]], w_out, out, f32, True, [a[-1] for a in afters] + tokens_out[:1])
        out = project(
            group[1:], [swap(second, 1)], w_out, out, bf16 if group == pairs_of[-1] else f32
        )
    return out, grad_query[0], *grads


def solution(mesh):
    nctx, nhead = mesh.shape["ctx"], mesh.shape["head"]
    return jax.shard_map(
        functools.partial(on_device, nctx, nhead),
        mesh=mesh,
        in_specs=(
            P("ctx", "head"),
            P("ctx", "head"),
            P("ctx", "head"),
            P("head"),
            P(),
            P(("ctx", "head"), None),
        ),
        out_specs=(P(("ctx", "head"), None), P("ctx", "head"), P("ctx", "head"), P("ctx", "head")),
        check_vma=False,
    )
```
